512 devices in a mesh: space: 8 (over y), chan: 16 (over x, z_lo, core), rep: 4 (over z_hi).
Axes of the slice: x: 4, y: 8, z: 8 (z_hi: 4, z_lo: 2; z = z_hi * 2 + z_lo), core: 2. Of those that a mesh axis runs over, the one named last changes fastest.
Arguments:
- volume: bfloat16 [4, 192, 8, 1024], P('rep', 'chan', 'space'), may hold values from -6 to 6
- weights: bfloat16 [27, 192, 192], replicated, may hold values from -0.078125 to 0.078125
- grad_out: bfloat16 [4, 192, 8, 1024], P('rep', 'chan', 'space'), may hold values from -6 to 6
Outputs:
- conv_out: bfloat16 [4, 192, 8, 1024], P('rep', 'chan', 'space')
- grad_in: bfloat16 [4, 192, 8, 1024], P('rep', 'chan', 'space')
- grad_weights: bfloat16 [27, 192, 192], P(None, None, 'chan')
The draws below stay inside these ranges and needn't reach their ends.
All inputs are finite; a program needn't handle non-finite values.
Results may differ from the reference program's by a relative error of at most 0.0014.
Values may be sent and summed in bfloat16 or wider, within the bound.
A program may use at most 64 MiB of HBM per device.

```python
import math
import jax
import jax.numpy as jnp
from jax import lax

C = 192
H = 32
W = 32
TAPS = 27
NB = 4
NZ = 8


def block_levels(rng, dims, split, low, largest):
    def one(axis_at, blocks):
        steps = jax.random.uniform(jax.random.fold_in(jax.random.fold_in(rng, 6), axis_at), (blocks,), jnp.float32, low / len(split), largest / len(split))
        return jnp.repeat(jnp.exp(steps), dims[axis_at] // blocks).reshape((-1,) + (1,) * (len(dims) - axis_at - 1))

    gain = one(*split[0])
    for cut in split[1:]:
        gain = gain * one(*cut)
    return gain


def noise(rng, extent, width, reach, split=(), held_as=jnp.bfloat16):
    level = block_levels(rng, extent, split, -0.22, 0.18) if split else 1.0
    drawn = jax.random.normal(rng, extent, jnp.float32) * width * level
    return jnp.minimum(jnp.maximum(drawn, -reach), reach).astype(held_as)


def setup_inputs(seed: int = 0) -> dict:
    streams_of = jax.random.split(jax.random.key(seed), 4)
    return {
        "volume": noise(streams_of[0], (NB, C, NZ, H * W), 1.0, 6.0, ((0, 4), (1, 16), (2, 8))),
        "weights": noise(streams_of[1], (TAPS, C, C), (27 * C) ** -0.5, 0.078125),
        "grad_out": noise(streams_of[2], (NB, C, NZ, H * W), 1.0, 6.0, ((0, 4), (1, 16), (2, 8))),
    }


OFFSETS = (-1, 0, 1)

def reference(volume, weights, grad_out):
    volume_f = volume.astype(jnp.float32).reshape(NB, C, NZ, H, W)
    grad_f = grad_out.astype(jnp.float32).reshape(NB, C, NZ, H, W)
    weight_f = weights.astype(jnp.float32)
    conv_sum = jnp.zeros((NB, C, NZ, H, W), jnp.float32)
    back_sum = jnp.zeros((NB, C, NZ, H, W), jnp.float32)
    kernel_rows = []
    for depth_off in OFFSETS:
        for row_off in OFFSETS:
            for col_off in OFFSETS:
                tap_index = (depth_off + 1) * 9 + (row_off + 1) * 3 + (col_off + 1)
                moved_in = jnp.roll(volume_f, (-depth_off, -row_off, -col_off), axis=(2, 3, 4))
                conv_sum = conv_sum + jnp.einsum('ic,bizhw->bczhw', weight_f[tap_index], moved_in, precision=lax.Precision.HIGHEST)
                moved_grad = jnp.roll(grad_f, (depth_off, row_off, col_off), axis=(2, 3, 4))
                back_sum = back_sum + jnp.einsum('ic,bczhw->bizhw', weight_f[tap_index], moved_grad, precision=lax.Precision.HIGHEST)
                kernel_rows.append(jnp.einsum('bizhw,bczhw->ic', volume_f, moved_grad, precision=lax.Precision.HIGHEST))
    factor = 1.0 / math.sqrt(NB * NZ * H * W)
    grad_weights = (jnp.stack(kernel_rows) * factor).astype(jnp.bfloat16)
    conv_out = conv_sum.reshape(NB, C, NZ, H * W).astype(jnp.bfloat16)
    grad_in = back_sum.reshape(NB, C, NZ, H * W).astype(jnp.bfloat16)
    return (conv_out, grad_in, grad_weights)
```

```python
import math

import jax
import jax.numpy as jnp
from jax import lax
from jax.experimental import pallas as pl
from jax.experimental.pallas import tpu as pltpu
from jax.sharding import PartitionSpec as P

H = 32
W = 32
CELLS = H * W
C = 192
BLOCK = 12
SLOT = 16
CHAN = 16
SPACE = 8
REP = 4
TAPS = 27
MEMBERS = SPACE * REP
HALF = 168
FACTOR = 1.0 / math.sqrt(4 * 8 * 1024)
MESH = pl.DeviceIdType.MESH
F32 = jnp.float32
BF16 = jnp.bfloat16


def onehot(cond):
    return jnp.where(cond, 1.0, 0.0).astype(BF16)


def iota(shape, dim):
    return lax.broadcasted_iota(jnp.int32, shape, dim)


def shift_cols(x, by):
    if by == 0:
        return x
    col = iota(x.shape, 1) & (W - 1)
    if by > 0:
        return jnp.where(col == W - 1, pltpu.roll(x, W - 1, 1), pltpu.roll(x, CELLS - 1, 1))
    return jnp.where(col == 0, pltpu.roll(x, CELLS - (W - 1), 1), pltpu.roll(x, 1, 1))


def shift_rows(x, by):
    if by == 0:
        return x
    return pltpu.roll(x, (-by * W) % CELLS, 1)


def depth_sums(rows, fields, sign, depth_off):
    first = (depth_off + 1) * 9 * SLOT
    products = jnp.dot(rows[first : first + 9 * SLOT, :], fields, preferred_element_type=F32)
    total = None
    for row_off in (-1, 0, 1):
        line = None
        for col_off in (-1, 0, 1):
            at = ((row_off + 1) * 3 + col_off + 1) * SLOT
            term = shift_cols(products[at : at + SLOT], sign * col_off)
            line = term if line is None else line + term
        line = shift_rows(line, sign * row_off)
        total = line if total is None else total + line
    return total


def position(co, tap):
    upper = co >= 6
    return jnp.where(upper, HALF + (co - 6) * TAPS, co * TAPS) + tap


def kernel(
    vol_ref, w_ref, grad_ref,
    conv_ref, gin_ref, gw_ref,
    vols, grads, halo, w_vmem, w_out, w_in, cols, out_sums, in_sums, parts, got, final,
    w_sem, vs, vr, gs, gr, fvs, fvr, fgs, fgr, hs, hr, xs, xr, rs, rr, as_, ar,
):
    space = lax.axis_index("space")
    chan = lax.axis_index("chan")
    rep = lax.axis_index("rep")
    core = lax.rem(chan, 2)
    chip = chan // 2
    sibling = chan + 1 - 2 * core
    up = lax.rem(space + 1, SPACE)
    down = lax.rem(space + SPACE - 1, SPACE)

    def chip_at(dx, dz):
        return lax.rem(chip // 2 + dx, 4) * 2 + lax.rem(chip + dz, 2)

    offsets = [(dx, dz) for dx in range(4) for dz in range(2) if dx or dz]

    def member_at(rel):
        return lax.rem(space + rel // REP, SPACE), lax.rem(rep + rel % REP, REP)

    w_copy = pltpu.make_async_copy(w_ref, w_vmem, w_sem)
    w_copy.start()

    pad = jnp.zeros((SLOT - BLOCK, CELLS), F32)
    vols[chan] = jnp.concatenate([vol_ref[...].astype(F32), pad], axis=0).astype(BF16)
    own_grad = jnp.concatenate([grad_ref[...].astype(F32), pad], axis=0)
    grads[chan] = own_grad.astype(BF16)

    barrier = pltpu.get_barrier_semaphore()
    for dx, dz in offsets:
        pl.semaphore_signal(
            barrier, inc=1, device_id={"chan": chip_at(dx, dz) * 2 + core}, device_id_type=MESH
        )
    pl.semaphore_signal(barrier, inc=1, device_id={"chan": sibling}, device_id_type=MESH)
    for rel in range(1, MEMBERS):
        y, z = member_at(rel)
        pl.semaphore_signal(barrier, inc=1, device_id={"space": y, "rep": z}, device_id_type=MESH)
    pl.semaphore_wait(barrier, 7 + 1 + MEMBERS - 1)

    def send(src, dst, s_sem, r_sem, where):
        return pltpu.make_async_remote_copy(
            src_ref=src, dst_ref=dst, send_sem=s_sem, recv_sem=r_sem,
            device_id=where, device_id_type=MESH,
        )

    halo_up = send(grads.at[chan], halo.at[0], hs.at[0], hr.at[0], {"space": up})
    halo_down = send(grads.at[chan], halo.at[1], hs.at[1], hr.at[1], {"space": down})
    halo_up.start()
    halo_down.start()

    def gather_starts(buf, s_sem, r_sem, fs_sem, fr_sem):
        copies = []
        for j, (dx, dz) in enumerate(offsets):
            c = send(buf.at[chan], buf.at[chan], s_sem.at[j], r_sem.at[j],
                     {"chan": chip_at(dx, dz) * 2 + core})
            c.start()
            copies.append(c)
        own = send(buf.at[chan], buf.at[chan], fs_sem.at[7], fr_sem.at[7], {"chan": sibling})
        own.start()
        return copies, own

    def gather_finish(buf, copies, own, fs_sem, fr_sem, r_sem, s_sem):
        forwards = []
        for j, (dx, dz) in enumerate(offsets):
            source = chip_at(4 - dx, 2 - dz) * 2 + core
            send(buf.at[source], buf.at[source], s_sem.at[j], r_sem.at[j],
                 {"chan": source}).wait_recv()
            f = send(buf.at[source], buf.at[source], fs_sem.at[j], fr_sem.at[j], {"chan": sibling})
            f.start()
            forwards.append(f)
        for j, (dx, dz) in enumerate(offsets):
            source = chip_at(4 - dx, 2 - dz) * 2 + 1 - core
            send(buf.at[source], buf.at[source], fs_sem.at[j], fr_sem.at[j],
                 {"chan": sibling}).wait_recv()
        send(buf.at[sibling], buf.at[sibling], fs_sem.at[7], fr_sem.at[7],
             {"chan": sibling}).wait_recv()
        return forwards

    v_copies, v_own = gather_starts(vols, vs, vr, fvs, fvr)
    g_copies, g_own = gather_starts(grads, gs, gr, fgs, fgr)

    lane = iota((C, CHAN * SLOT), 1)
    slot_of = onehot(
        ((lane >> 4) * BLOCK + (lane & 15) == iota((C, CHAN * SLOT), 0)) & ((lane & 15) < BLOCK)
    )
    row = iota((SLOT, C), 0)
    mine = onehot((iota((SLOT, C), 1) == chan * BLOCK + row) & (row < BLOCK))
    col = iota((2 * HALF, TAPS * SLOT), 1)
    order = onehot(
        (position(col & 15, col >> 4) == iota((2 * HALF, TAPS * SLOT), 0)) & ((col & 15) < BLOCK)
    )

    halo_up.wait_recv()
    halo_down.wait_recv()
    for depth_off in (-1, 0, 1):
        plane = own_grad if depth_off == 0 else halo[(1 - depth_off) // 2].astype(F32)
        for col_off in (-1, 0, 1):
            moved = shift_cols(plane, -col_off)
            for row_off in (-1, 0, 1):
                tap = (depth_off + 1) * 9 + (row_off + 1) * 3 + col_off + 1
                cols[tap * SLOT : (tap + 1) * SLOT, :] = shift_rows(moved, -row_off).astype(BF16)
    ordered = jnp.dot(order, cols[...], preferred_element_type=F32).astype(BF16)

    w_copy.wait()
    for tap in range(TAPS):
        at = slice(tap * SLOT, (tap + 1) * SLOT)
        w_in[at, :] = jnp.dot(
            jnp.dot(mine, w_vmem[tap], preferred_element_type=F32).astype(BF16), slot_of,
            preferred_element_type=F32,
        ).astype(BF16)
        w_out[at, :] = jnp.dot(
            lax.dot_general(
                mine, w_vmem[tap], (((1,), (1,)), ((), ())), preferred_element_type=F32
            ).astype(BF16), slot_of, preferred_element_type=F32,
        ).astype(BF16)

    v_forwards = gather_finish(vols, v_copies, v_own, fvs, fvr, vr, vs)
    fields = vols[...].reshape(CHAN * SLOT, CELLS)
    packed = jnp.dot(slot_of, fields, preferred_element_type=F32).astype(BF16)
    sums = lax.dot_general(
        ordered, packed, (((1,), (1,)), ((), ())), preferred_element_type=F32
    )
    parts[0:21] = sums[:, :128].reshape(21, 16, 128)
    side = jnp.concatenate([sums[:HALF, 128:], sums[HALF:, 128:]], axis=1)
    side = jnp.concatenate([side, jnp.zeros((8, 128), F32)], axis=0)
    parts[21:32] = side.reshape(11, 16, 128)

    scatters = []
    for rel in range(1, MEMBERS):
        y, z = member_at(rel)
        c = send(parts.at[y * REP + z], got.at[rel - 1], rs.at[rel - 1], rr.at[rel - 1],
                 {"space": y, "rep": z})
        c.start()
        scatters.append(c)

    exchanges = []

    def exchange(slot, buf, side_at, where):
        c = send(buf.at[side_at], buf.at[side_at + 2], xs.at[slot], xr.at[slot], {"space": where})
        c.start()
        exchanges.append(c)

    out_sums[0] = depth_sums(w_out, fields, 1, 1)
    exchange(0, out_sums, 0, down)
    out_sums[1] = depth_sums(w_out, fields, 1, -1)
    exchange(1, out_sums, 1, up)
    out_sums[4] = depth_sums(w_out, fields, 1, 0)

    g_forwards = gather_finish(grads, g_copies, g_own, fgs, fgr, gr, gs)
    grad_fields = grads[...].reshape(CHAN * SLOT, CELLS)
    in_sums[0] = depth_sums(w_in, grad_fields, -1, 1)
    exchange(2, in_sums, 0, up)
    in_sums[1] = depth_sums(w_in, grad_fields, -1, -1)
    exchange(3, in_sums, 1, down)

    me = space * REP + rep
    total = parts[me]
    for rel in range(1, MEMBERS):
        scatters[rel - 1].wait_recv()
        total = total + got[rel - 1]
    final[me] = (total * FACTOR).astype(BF16)
    gathers = []
    for rel in range(1, MEMBERS):
        y, z = member_at(rel)
        c = send(final.at[me], final.at[me], as_.at[rel - 1], ar.at[rel - 1],
                 {"space": y, "rep": z})
        c.start()
        gathers.append(c)

    in_sums[4] = depth_sums(w_in, grad_fields, -1, 0)
    q = iota((BLOCK * 32, 512), 0)
    at = position(q >> 5, q & 31)
    here = iota((BLOCK * 32, 512), 1)
    real = (q & 31) < TAPS
    low = onehot((at == here) & real)
    high = onehot((jnp.where(at >= HALF, at - HALF, at) + 2 * HALF == here) & real)

    for c in exchanges:
        c.wait_recv()
    conv_ref[...] = (out_sums[4] + out_sums[2] + out_sums[3])[:BLOCK].astype(BF16)
    gin_ref[...] = (in_sums[4] + in_sums[2] + in_sums[3])[:BLOCK].astype(BF16)

    for rel in range(1, MEMBERS):
        src = lax.rem(space + SPACE - rel // REP, SPACE) * REP + lax.rem(rep + REP - rel % REP, REP)
        send(final.at[src], final.at[src], as_.at[rel - 1], ar.at[rel - 1],
             {"space": up}).wait_recv()
    table = final[...].reshape(512, 128)
    left = jnp.dot(low, table, preferred_element_type=F32).astype(BF16)
    right = jnp.dot(high, table, preferred_element_type=F32)
    rows = 6 * 32
    right = jnp.concatenate([right[:rows, :64], right[rows:, 64:]], axis=0).astype(BF16)
    gw_ref[:, :, 0:128] = left.reshape(BLOCK, 32, 128)[:, :TAPS, :]
    gw_ref[:, :, 128:192] = right.reshape(BLOCK, 32, 64)[:, :TAPS, :]

    for c in (v_copies + g_copies + [v_own, g_own, halo_up, halo_down] + v_forwards
              + g_forwards + scatters + exchanges + gathers):
        c.wait_send()


def on_device(volume, weights, grad_out):
    vmem = pl.BlockSpec(memory_space=pltpu.VMEM)
    dma = pltpu.SemaphoreType.DMA
    conv, gin, gw = pl.pallas_call(
        kernel,
        out_shape=(
            jax.ShapeDtypeStruct((BLOCK, CELLS), BF16),
            jax.ShapeDtypeStruct((BLOCK, CELLS), BF16),
            jax.ShapeDtypeStruct((BLOCK, TAPS, C), BF16),
        ),
        in_specs=[vmem, pl.BlockSpec(memory_space=pl.ANY), vmem],
        out_specs=(vmem, vmem, vmem),
        scratch_shapes=[
            pltpu.VMEM((CHAN, SLOT, CELLS), BF16),
            pltpu.VMEM((CHAN, SLOT, CELLS), BF16),
            pltpu.VMEM((2, SLOT, CELLS), BF16),
            pltpu.VMEM((TAPS, C, C), BF16),
            pltpu.VMEM((TAPS * SLOT, CHAN * SLOT), BF16),
            pltpu.VMEM((TAPS * SLOT, CHAN * SLOT), BF16),
            pltpu.VMEM((TAPS * SLOT, CELLS), BF16),
            pltpu.VMEM((5, SLOT, CELLS), F32),
            pltpu.VMEM((5, SLOT, CELLS), F32),
            pltpu.VMEM((MEMBERS, 16, 128), F32),
            pltpu.VMEM((MEMBERS - 1, 16, 128), F32),
            pltpu.VMEM((MEMBERS, 16, 128), BF16),
            dma,
            dma((7,)), dma((7,)), dma((7,)), dma((7,)),
            dma((8,)), dma((8,)), dma((8,)), dma((8,)),
            dma((2,)), dma((2,)), dma((4,)), dma((4,)),
            dma((MEMBERS - 1,)), dma((MEMBERS - 1,)), dma((MEMBERS - 1,)), dma((MEMBERS - 1,)),
        ],
        compiler_params=pltpu.CompilerParams(
            collective_id=0, has_side_effects=True, vmem_limit_bytes=48 * 1024 * 1024
        ),
        cost_estimate=pl.CostEstimate(
            flops=400_000_000, bytes_accessed=3_000_000, transcendentals=0
        ),
    )(volume.reshape(BLOCK, CELLS), weights, grad_out.reshape(BLOCK, CELLS))
    shape = volume.shape
    return conv.reshape(shape), gin.reshape(shape), jnp.transpose(gw, (1, 2, 0))


def solution(mesh):
    return jax.shard_map(
        on_device,
        mesh=mesh,
        in_specs=(P("rep", "chan", "space", None), P(), P("rep", "chan", "space", None)),
        out_specs=(
            P("rep", "chan", "space", None),
            P("rep", "chan", "space", None),
            P(None, None, "chan"),
        ),
        check_vma=False,
    )
```

```python
import math

import jax
import jax.numpy as jnp
from jax import lax
from jax.experimental import pallas as pl
from jax.experimental.pallas import tpu as pltpu
from jax.sharding import PartitionSpec as P

H = 32
W = 32
CELLS = H * W
C = 192
BLOCK = 12
SLOT = 16
CHAN = 16
SPACE = 8
REP = 4
TAPS = 27
MEMBERS = SPACE * REP
MAIN = 243
SIDE = 81
FACTOR = 1.0 / math.sqrt(4 * 8 * 1024)
MESH = pl.DeviceIdType.MESH
F32 = jnp.float32
BF16 = jnp.bfloat16
FIRST = ((0, 1), (1, 0), (1, 1))
SECOND = ((3, 0), (3, 1), (2, 0), (2, 1))


def onehot(cond):
    return jnp.where(cond, 1.0, 0.0).astype(BF16)


def iota(shape, dim):
    return lax.broadcasted_iota(jnp.int32, shape, dim)


def dot(a, b):
    return jnp.dot(a, b, preferred_element_type=F32)


def dot_nt(a, b):
    return lax.dot_general(a, b, (((1,), (1,)), ((), ())), preferred_element_type=F32)


def shift_cols(x, by):
    if by == 0:
        return x
    col = iota(x.shape, 1) & (W - 1)
    if by > 0:
        return jnp.where(col == W - 1, pltpu.roll(x, W - 1, 1), pltpu.roll(x, CELLS - 1, 1))
    return jnp.where(col == 0, pltpu.roll(x, CELLS - (W - 1), 1), pltpu.roll(x, 1, 1))


def shift_rows(x, by):
    if by == 0:
        return x
    return pltpu.roll(x, (-by * W) % CELLS, 1)


def depth_sums(rows, fields, sign, depth_off):
    first = (depth_off + 1) * 9 * SLOT
    products = dot(rows[first : first + 9 * SLOT, :], fields)
    total = None
    for row_off in (-1, 0, 1):
        line = None
        for col_off in (-1, 0, 1):
            at = ((row_off + 1) * 3 + col_off + 1) * SLOT
            term = shift_cols(products[at : at + SLOT], sign * col_off)
            line = term if line is None else line + term
        line = shift_rows(line, sign * row_off)
        total = line if total is None else total + line
    return total


def divide(x, by, below):
    out = jnp.zeros_like(x)
    for k in range(by, below, by):
        out = out + jnp.where(x >= k, 1, 0)
    return out


def kernel(
    vol_ref, w_ref, grad_ref,
    conv_ref, gin_ref, gw_ref,
    vol_in, grad_in, vols, grads, halo, w_vmem, w_out, w_in, cols, out_sums, in_sums,
    parts, got, final,
    in_sem, vs, vr, gs, gr, fvs, fvr, fgs, fgr, hs, hr, xs, xr, rs, rr, as_, ar,
):
    space = lax.axis_index("space")
    chan = lax.axis_index("chan")
    rep = lax.axis_index("rep")
    core = lax.rem(chan, 2)
    z_lo = lax.rem(chan // 2, 2)
    x_at = chan // 4
    sibling = chan + 1 - 2 * core
    up = lax.rem(space + 1, SPACE)
    down = lax.rem(space + SPACE - 1, SPACE)
    me = space * REP + rep

    vol_copy = pltpu.make_async_copy(vol_ref, vol_in, in_sem.at[0])
    grad_copy = pltpu.make_async_copy(grad_ref, grad_in, in_sem.at[1])
    w_copy = pltpu.make_async_copy(w_ref, w_vmem, in_sem.at[2])
    vol_copy.start()
    grad_copy.start()
    w_copy.start()

    def chip_at(dx, dz):
        return lax.rem(x_at + dx, 4) * 4 + lax.rem(z_lo + dz, 2) * 2 + core

    barrier = pltpu.get_barrier_semaphore()
    for dx, dz in FIRST + SECOND:
        pl.semaphore_signal(barrier, inc=1, device_id={"chan": chip_at(dx, dz)}, device_id_type=MESH)
    pl.semaphore_signal(barrier, inc=1, device_id={"chan": sibling}, device_id_type=MESH)
    for rel in range(1, MEMBERS):
        pl.semaphore_signal(
            barrier, inc=1,
            device_id={
                "space": lax.rem(space + rel // REP, SPACE), "rep": lax.rem(rep + rel % REP, REP)
            },
            device_id_type=MESH,
        )

    pad = jnp.zeros((SLOT - BLOCK, CELLS), F32)
    vol_copy.wait()
    vols[0] = jnp.concatenate([vol_in[...].astype(F32), pad], axis=0).astype(BF16)
    grad_copy.wait()
    own_grad = jnp.concatenate([grad_in[...].astype(F32), pad], axis=0)
    grads[0] = own_grad.astype(BF16)
    pl.semaphore_wait(barrier, 7 + 1 + MEMBERS - 1)

    def send(src, dst, s_sem, r_sem, where):
        return pltpu.make_async_remote_copy(
            src_ref=src, dst_ref=dst, send_sem=s_sem, recv_sem=r_sem,
            device_id=where, device_id_type=MESH,
        )

    def to_peer(buf, dx, dz, s_sem, r_sem):
        slot = dx * 4 + dz * 2
        return send(buf.at[0], buf.at[slot], s_sem.at[slot // 2], r_sem.at[slot // 2],
                    {"chan": chip_at(4 - dx, dz)})

    def to_sibling(buf, dx, dz, s_sem, r_sem):
        slot = dx * 4 + dz * 2
        return send(buf.at[slot], buf.at[slot + 1], s_sem.at[slot // 2], r_sem.at[slot // 2],
                    {"chan": sibling})

    started = []

    def go(copy):
        copy.start()
        started.append(copy)

    def pass_on(buf, group, sems):
        s_sem, r_sem, fs_sem, fr_sem = sems
        for dx, dz in group:
            to_peer(buf, dx, dz, s_sem, r_sem).wait_recv()
            go(to_sibling(buf, dx, dz, fs_sem, fr_sem))
        for dx, dz in group:
            to_sibling(buf, dx, dz, fs_sem, fr_sem).wait_recv()

    v_sems = (vs, vr, fvs, fvr)
    g_sems = (gs, gr, fgs, fgr)
    for dx, dz in FIRST:
        go(to_peer(vols, dx, dz, vs, vr))
    go(to_sibling(vols, 0, 0, fvs, fvr))
    halo_up = send(grads.at[0], halo.at[0], hs.at[0], hr.at[0], {"space": up})
    halo_down = send(grads.at[0], halo.at[1], hs.at[1], hr.at[1], {"space": down})
    go(halo_up)
    go(halo_down)
    for dx, dz in SECOND:
        go(to_peer(vols, dx, dz, vs, vr))

    row = iota((328, TAPS * SLOT), 0)
    col = iota((328, TAPS * SLOT), 1)
    order = onehot(((col & 15) * TAPS + (col >> 4) == row) & ((col & 15) < BLOCK))
    row = iota((96, 128), 0)
    col = iota((96, 128), 1)
    compact = onehot(((col >> 4) * BLOCK + (col & 15) == row) & ((col & 15) < BLOCK))

    def columns(depth_off, plane):
        for col_off in (-1, 0, 1):
            moved = shift_cols(plane, -col_off)
            for row_off in (-1, 0, 1):
                tap = (depth_off + 1) * 9 + (row_off + 1) * 3 + col_off + 1
                cols[tap * SLOT : (tap + 1) * SLOT, :] = shift_rows(moved, -row_off).astype(BF16)

    columns(0, own_grad)
    halo_up.wait_recv()
    columns(1, halo[0].astype(F32))
    halo_down.wait_recv()
    columns(-1, halo[1].astype(F32))
    ordered = dot(order, cols[...]).astype(BF16)

    def scatter(half):
        fields = vols[8 * half : 8 * half + 8].reshape(8 * SLOT, CELLS)
        packed = dot(compact, fields).astype(BF16)
        sums = dot_nt(ordered, packed)
        side = sums[MAIN : MAIN + SIDE]
        side = jnp.concatenate(
            [side[:, 0:32], side[:, 32:64], side[:, 64:96], jnp.zeros((13, 32), F32)], axis=0
        )
        parts[16 * half : 16 * half + 16] = jnp.concatenate([sums[:256], side], axis=1).reshape(
            16, 16, 128
        )
        for k in range(4):
            pair = lax.rem(space // 2 + k, 4)
            for dz in range(REP):
                y, z = 2 * pair + half, lax.rem(rep + dz, REP)
                copy = send(parts.at[16 * half + pair * REP + z], got.at[me], rs, rr,
                            {"space": y, "rep": z})
                if k == 0 and dz == 0:
                    pl.when(y != space)(copy.start)
                else:
                    copy.start()

    to_sibling(vols, 0, 0, fvs, fvr).wait_recv()
    pass_on(vols, FIRST, v_sems)
    scatter(0)
    pass_on(vols, SECOND, v_sems)
    scatter(1)

    for dx, dz in FIRST + SECOND:
        go(to_peer(grads, dx, dz, gs, gr))
    go(to_sibling(grads, 0, 0, fgs, fgr))

    lane = iota((C, CHAN * SLOT), 1)
    at_x = (x_at + (lane >> 6)) & 3
    at_z = (z_lo + (lane >> 5)) & 1
    at_core = (core + (lane >> 4)) & 1
    block = (at_x * 4 + at_z * 2 + at_core) * BLOCK
    slot_of = onehot((block + (lane & 15) == iota((C, CHAN * SLOT), 0)) & ((lane & 15) < BLOCK))
    row = iota((SLOT, C), 0)
    mine = onehot((iota((SLOT, C), 1) == chan * BLOCK + row) & (row < BLOCK))
    w_copy.wait()
    picked = [dot_nt(mine, w_vmem[tap]).astype(BF16) for tap in range(TAPS)]
    w_out[...] = dot(jnp.concatenate(picked, axis=0), slot_of).astype(BF16)

    def exchange(slot, buf, side_at, where):
        go(send(buf.at[side_at], buf.at[side_at + 2], xs.at[slot], xr.at[slot], {"space": where}))

    fields = vols[...].reshape(CHAN * SLOT, CELLS)
    out_sums[0] = depth_sums(w_out, fields, 1, 1)
    exchange(0, out_sums, 0, down)
    out_sums[1] = depth_sums(w_out, fields, 1, -1)
    exchange(1, out_sums, 1, up)

    piece = lax.rem(space, 2) * 16 + (space // 2) * REP + rep
    got[me] = parts[piece]
    bulk = pl.ds(0, MEMBERS - 1)
    send(got.at[bulk], got.at[bulk], rs, rr, {"space": up}).wait_recv()
    final[piece] = (jnp.sum(got[...], axis=0) * FACTOR).astype(BF16)
    for rel in range(1, MEMBERS):
        send(final.at[piece], final.at[piece], as_, ar, {
            "space": lax.rem(space + rel // REP, SPACE), "rep": lax.rem(rep + rel % REP, REP)
        }).start()

    picked = [dot(mine, w_vmem[tap]).astype(BF16) for tap in range(TAPS)]
    w_in[...] = dot(jnp.concatenate(picked, axis=0), slot_of).astype(BF16)
    to_sibling(grads, 0, 0, fgs, fgr).wait_recv()
    pass_on(grads, FIRST + SECOND, g_sems)
    grad_fields = grads[...].reshape(CHAN * SLOT, CELLS)
    in_sums[0] = depth_sums(w_in, grad_fields, -1, 1)
    exchange(2, in_sums, 0, up)
    in_sums[1] = depth_sums(w_in, grad_fields, -1, -1)
    exchange(3, in_sums, 1, down)
    out_sums[4] = depth_sums(w_out, fields, 1, 0)
    in_sums[4] = depth_sums(w_in, grad_fields, -1, 0)

    row = iota((9 * 32, 256), 0)
    main_rows = onehot(
        ((row >> 5) * TAPS + (row & 31) == iota((9 * 32, 256), 1)) & ((row & 31) < TAPS)
    )
    row = iota((3 * 32, 256), 0)
    side_at = (row >> 5) * TAPS + (row & 31)
    side_rows = [
        onehot((side_at + SIDE * j == iota((3 * 32, 256), 1)) & ((row & 31) < TAPS))
        for j in range(3)
    ]

    def lanes(half, index):
        slot = divide(index, BLOCK, 96)
        to_x = (x_at + 2 * half + (slot >> 2)) & 3
        to_z = (z_lo + (slot >> 1)) & 1
        to_core = (core + slot) & 1
        return (to_x * 4 + to_z * 2 + to_core) * BLOCK + index - slot * BLOCK

    lane = iota((128, 1), 0)
    target = iota((128, C), 1)
    main_lanes = [onehot((lanes(h, lane) == target) & (lane < 96)) for h in range(2)]
    side_lanes = [
        [onehot((lanes(h, jnp.maximum(lane - 96, 0) + 32 * j) == target) & (lane >= 96))
         for j in range(3)]
        for h in range(2)
    ]

    for slot, buf in ((0, out_sums), (1, out_sums), (2, in_sums), (3, in_sums)):
        side = slot % 2
        send(buf.at[side], buf.at[side + 2], xs.at[slot], xr.at[slot], {"space": up}).wait_recv()
    conv_ref[...] = (out_sums[4] + out_sums[2] + out_sums[3])[:BLOCK].astype(BF16)
    gin_ref[...] = (in_sums[4] + in_sums[2] + in_sums[3])[:BLOCK].astype(BF16)

    send(final.at[bulk], final.at[bulk], as_, ar, {"space": up}).wait_recv()
    main = jnp.zeros((9 * 32, C), F32)
    side = jnp.zeros((3 * 32, C), F32)
    for h in range(2):
        table = final[16 * h : 16 * h + 16].reshape(256, 128)
        main = main + dot(dot(main_rows, table).astype(BF16), main_lanes[h])
        for j in range(3):
            side = side + dot(dot(side_rows[j], table).astype(BF16), side_lanes[h][j])
    gw_ref[0:9] = main.astype(BF16).reshape(9, 32, C)[:, :TAPS, :]
    gw_ref[9:12] = side.astype(BF16).reshape(3, 32, C)[:, :TAPS, :]

    for copy in started:
        copy.wait_send()
    send(got.at[bulk], got.at[bulk], rs, rr, {"space": up}).wait_send()
    send(final.at[bulk], final.at[bulk], as_, ar, {"space": up}).wait_send()


def on_device(volume, weights, grad_out):
    vmem = pl.BlockSpec(memory_space=pltpu.VMEM)
    hbm = pl.BlockSpec(memory_space=pltpu.HBM)
    dma = pltpu.SemaphoreType.DMA
    conv, gin, gw = pl.pallas_call(
        kernel,
        out_shape=(
            jax.ShapeDtypeStruct((BLOCK, CELLS), BF16),
            jax.ShapeDtypeStruct((BLOCK, CELLS), BF16),
            jax.ShapeDtypeStruct((BLOCK, TAPS, C), BF16),
        ),
        in_specs=[hbm, hbm, hbm],
        out_specs=(vmem, vmem, vmem),
        scratch_shapes=[
            pltpu.VMEM((BLOCK, CELLS), BF16),
            pltpu.VMEM((BLOCK, CELLS), BF16),
            pltpu.VMEM((CHAN, SLOT, CELLS), BF16),
            pltpu.VMEM((CHAN, SLOT, CELLS), BF16),
            pltpu.VMEM((2, SLOT, CELLS), BF16),
            pltpu.VMEM((TAPS, C, C), BF16),
            pltpu.VMEM((TAPS * SLOT, CHAN * SLOT), BF16),
            pltpu.VMEM((TAPS * SLOT, CHAN * SLOT), BF16),
            pltpu.VMEM((TAPS * SLOT, CELLS), BF16),
            pltpu.VMEM((5, SLOT, CELLS), F32),
            pltpu.VMEM((5, SLOT, CELLS), F32),
            pltpu.VMEM((MEMBERS, 16, 128), F32),
            pltpu.VMEM((MEMBERS, 16, 128), F32),
            pltpu.VMEM((MEMBERS, 16, 128), BF16),
            dma((3,)),
            dma((8,)), dma((8,)), dma((8,)), dma((8,)),
            dma((8,)), dma((8,)), dma((8,)), dma((8,)),
            dma((2,)), dma((2,)), dma((4,)), dma((4,)),
            dma, dma, dma, dma,
        ],
        compiler_params=pltpu.CompilerParams(
            collective_id=0, has_side_effects=True, vmem_limit_bytes=40 * 1024 * 1024
        ),
        cost_estimate=pl.CostEstimate(
            flops=400_000_000, bytes_accessed=3_000_000, transcendentals=0
        ),
    )(volume.reshape(BLOCK, CELLS), weights, grad_out.reshape(BLOCK, CELLS))
    shape = volume.shape
    return conv.reshape(shape), gin.reshape(shape), jnp.transpose(gw, (1, 2, 0))


def solution(mesh):
    return jax.shard_map(
        on_device,
        mesh=mesh,
        in_specs=(P("rep", "chan", "space", None), P(), P("rep", "chan", "space", None)),
        out_specs=(
            P("rep", "chan", "space", None),
            P("rep", "chan", "space", None),
            P(None, None, "chan"),
        ),
        check_vma=False,
    )
```

```python
import math

import jax
import jax.numpy as jnp
from jax import lax
from jax.experimental import pallas as pl
from jax.experimental.pallas import tpu as pltpu
from jax.sharding import PartitionSpec as P

H = 32
W = 32
CELLS = H * W
C = 192
BLOCK = 12
SLOT = 16
CHAN = 16
SPACE = 8
REP = 4
TAPS = 27
MEMBERS = SPACE * REP
MAIN = 243
SIDE = 81
FACTOR = 1.0 / math.sqrt(4 * 8 * 1024)
MESH = pl.DeviceIdType.MESH
F32 = jnp.float32
BF16 = jnp.bfloat16
FIRST = ((0, 1), (1, 0), (1, 1))
SECOND = ((3, 0), (3, 1), (2, 0), (2, 1))


def onehot(cond):
    return jnp.where(cond, 1.0, 0.0).astype(BF16)


def iota(shape, dim):
    return lax.broadcasted_iota(jnp.int32, shape, dim)


def dot(a, b):
    return jnp.dot(a, b, preferred_element_type=F32)


def dot_nt(a, b):
    return lax.dot_general(a, b, (((1,), (1,)), ((), ())), preferred_element_type=F32)


def shift_cols(x, by):
    if by == 0:
        return x
    col = iota(x.shape, 1) & (W - 1)
    if by > 0:
        return jnp.where(col == W - 1, pltpu.roll(x, W - 1, 1), pltpu.roll(x, CELLS - 1, 1))
    return jnp.where(col == 0, pltpu.roll(x, CELLS - (W - 1), 1), pltpu.roll(x, 1, 1))


def shift_rows(x, by):
    if by == 0:
        return x
    return pltpu.roll(x, (-by * W) % CELLS, 1)


def depth_sums(rows, fields, sign, depth_off):
    first = (depth_off + 1) * 9 * SLOT
    products = dot(rows[first : first + 9 * SLOT, :], fields)
    total = None
    for row_off in (-1, 0, 1):
        line = None
        for col_off in (-1, 0, 1):
            at = ((row_off + 1) * 3 + col_off + 1) * SLOT
            term = shift_cols(products[at : at + SLOT], sign * col_off)
            line = term if line is None else line + term
        line = shift_rows(line, sign * row_off)
        total = line if total is None else total + line
    return total


def divide(x, by, below):
    out = jnp.zeros_like(x)
    for k in range(by, below, by):
        out = out + jnp.where(x >= k, 1, 0)
    return out


def kernel(
    vol_ref, w_ref, grad_ref,
    conv_ref, gin_ref, gw_ref,
    vol_in, grad_in, vols, grads, halo, w_vmem, w_out, w_in, cols, out_sums, in_sums,
    parts, got, final,
    in_sem, vs, vr, gs, gr, fvs, fvr, fgs, fgr, hs, hr, xs, xr, rs, rr, as_, ar,
):
    space = lax.axis_index("space")
    chan = lax.axis_index("chan")
    rep = lax.axis_index("rep")
    core = lax.rem(chan, 2)
    z_lo = lax.rem(chan // 2, 2)
    x_at = chan // 4
    sibling = chan + 1 - 2 * core
    up = lax.rem(space + 1, SPACE)
    down = lax.rem(space + SPACE - 1, SPACE)
    me = space * REP + rep

    vol_copy = pltpu.make_async_copy(vol_ref, vol_in, in_sem.at[0])
    grad_copy = pltpu.make_async_copy(grad_ref, grad_in, in_sem.at[1])
    w_copy = pltpu.make_async_copy(w_ref, w_vmem, in_sem.at[2])
    vol_copy.start()
    grad_copy.start()
    w_copy.start()

    def chip_at(dx, dz):
        return lax.rem(x_at + dx, 4) * 4 + lax.rem(z_lo + dz, 2) * 2 + core

    barrier = pltpu.get_barrier_semaphore()
    for dx, dz in FIRST + SECOND:
        pl.semaphore_signal(barrier, inc=1, device_id={"chan": chip_at(dx, dz)}, device_id_type=MESH)
    pl.semaphore_signal(barrier, inc=1, device_id={"chan": sibling}, device_id_type=MESH)
    for rel in range(1, MEMBERS):
        pl.semaphore_signal(
            barrier, inc=1,
            device_id={
                "space": lax.rem(space + rel // REP, SPACE), "rep": lax.rem(rep + rel % REP, REP)
            },
            device_id_type=MESH,
        )

    pad = jnp.zeros((SLOT - BLOCK, CELLS), F32)
    vol_copy.wait()
    vols[0] = jnp.concatenate([vol_in[...].astype(F32), pad], axis=0).astype(BF16)
    grad_copy.wait()
    own_grad = jnp.concatenate([grad_in[...].astype(F32), pad], axis=0)
    grads[0] = own_grad.astype(BF16)
    pl.semaphore_wait(barrier, 7 + 1 + MEMBERS - 1)

    def send(src, dst, s_sem, r_sem, where):
        return pltpu.make_async_remote_copy(
            src_ref=src, dst_ref=dst, send_sem=s_sem, recv_sem=r_sem,
            device_id=where, device_id_type=MESH,
        )

    def to_peer(buf, dx, dz, s_sem, r_sem):
        slot = dx * 4 + dz * 2
        return send(buf.at[0], buf.at[slot], s_sem.at[slot // 2], r_sem.at[slot // 2],
                    {"chan": chip_at(4 - dx, dz)})

    def to_sibling(buf, dx, dz, s_sem, r_sem):
        slot = dx * 4 + dz * 2
        return send(buf.at[slot], buf.at[slot + 1], s_sem.at[slot // 2], r_sem.at[slot // 2],
                    {"chan": sibling})

    started = []

    def go(copy):
        copy.start()
        started.append(copy)

    def pass_on(buf, group, sems):
        s_sem, r_sem, fs_sem, fr_sem = sems
        for dx, dz in group:
            to_peer(buf, dx, dz, s_sem, r_sem).wait_recv()
            go(to_sibling(buf, dx, dz, fs_sem, fr_sem))
        for dx, dz in group:
            to_sibling(buf, dx, dz, fs_sem, fr_sem).wait_recv()

    v_sems = (vs, vr, fvs, fvr)
    g_sems = (gs, gr, fgs, fgr)
    for dx, dz in FIRST:
        go(to_peer(vols, dx, dz, vs, vr))
    go(to_sibling(vols, 0, 0, fvs, fvr))
    halo_up = send(grads.at[0], halo.at[0], hs.at[0], hr.at[0], {"space": up})
    halo_down = send(grads.at[0], halo.at[1], hs.at[1], hr.at[1], {"space": down})
    go(halo_up)
    go(halo_down)
    for dx, dz in SECOND:
        go(to_peer(vols, dx, dz, vs, vr))
    for dx, dz in FIRST + SECOND:
        go(to_peer(grads, dx, dz, gs, gr))
    go(to_sibling(grads, 0, 0, fgs, fgr))

    row = iota((328, TAPS * SLOT), 0)
    col = iota((328, TAPS * SLOT), 1)
    order = onehot(((col & 15) * TAPS + (col >> 4) == row) & ((col & 15) < BLOCK))
    row = iota((96, 128), 0)
    col = iota((96, 128), 1)
    compact = onehot(((col >> 4) * BLOCK + (col & 15) == row) & ((col & 15) < BLOCK))

    def columns(depth_off, plane):
        for col_off in (-1, 0, 1):
            moved = shift_cols(plane, -col_off)
            for row_off in (-1, 0, 1):
                tap = (depth_off + 1) * 9 + (row_off + 1) * 3 + col_off + 1
                cols[tap * SLOT : (tap + 1) * SLOT, :] = shift_rows(moved, -row_off).astype(BF16)

    columns(0, own_grad)
    halo_up.wait_recv()
    columns(1, halo[0].astype(F32))
    halo_down.wait_recv()
    columns(-1, halo[1].astype(F32))
    ordered = dot(order, cols[...]).astype(BF16)

    def scatter(half):
        fields = vols[8 * half : 8 * half + 8].reshape(8 * SLOT, CELLS)
        packed = dot(compact, fields).astype(BF16)
        sums = dot_nt(ordered, packed)
        side = sums[MAIN : MAIN + SIDE]
        side = jnp.concatenate(
            [side[:, 0:32], side[:, 32:64], side[:, 64:96], jnp.zeros((13, 32), F32)], axis=0
        )
        parts[16 * half : 16 * half + 16] = jnp.concatenate([sums[:256], side], axis=1).reshape(
            16, 16, 128
        )
        for k in range(4):
            pair = lax.rem(space // 2 + k, 4)
            for dz in range(REP):
                y, z = 2 * pair + half, lax.rem(rep + dz, REP)
                copy = send(parts.at[16 * half + pair * REP + z], got.at[me], rs, rr,
                            {"space": y, "rep": z})
                if k == 0 and dz == 0:
                    pl.when(y != space)(copy.start)
                else:
                    copy.start()

    to_sibling(vols, 0, 0, fvs, fvr).wait_recv()
    pass_on(vols, FIRST, v_sems)
    scatter(0)
    lane = iota((C, CHAN * SLOT), 1)
    at_x = (x_at + (lane >> 6)) & 3
    at_z = (z_lo + (lane >> 5)) & 1
    at_core = (core + (lane >> 4)) & 1
    block = (at_x * 4 + at_z * 2 + at_core) * BLOCK
    slot_of = onehot((block + (lane & 15) == iota((C, CHAN * SLOT), 0)) & ((lane & 15) < BLOCK))
    row = iota((SLOT, C), 0)
    mine = onehot((iota((SLOT, C), 1) == chan * BLOCK + row) & (row < BLOCK))
    w_copy.wait()
    picked = [dot_nt(mine, w_vmem[tap]).astype(BF16) for tap in range(TAPS)]
    w_out[...] = dot(jnp.concatenate(picked, axis=0), slot_of).astype(BF16)
    pass_on(vols, SECOND, v_sems)
    scatter(1)
    picked = [dot(mine, w_vmem[tap]).astype(BF16) for tap in range(TAPS)]
    w_in[...] = dot(jnp.concatenate(picked, axis=0), slot_of).astype(BF16)

    piece = lax.rem(space, 2) * 16 + (space // 2) * REP + rep
    bulk = pl.ds(0, MEMBERS - 1)

    def reduce_piece():
        got[me] = parts[piece]
        send(got.at[bulk], got.at[bulk], rs, rr, {"space": up}).wait_recv()
        final[piece] = (jnp.sum(got[...], axis=0) * FACTOR).astype(BF16)
        for rel in range(1, MEMBERS):
            send(final.at[piece], final.at[piece], as_, ar, {
                "space": lax.rem(space + rel // REP, SPACE), "rep": lax.rem(rep + rel % REP, REP)
            }).start()

    even = lax.rem(space, 2) == 0
    pl.when(even)(reduce_piece)


    def exchange(slot, buf, side_at, where):
        go(send(buf.at[side_at], buf.at[side_at + 2], xs.at[slot], xr.at[slot], {"space": where}))

    fields = vols[...].reshape(CHAN * SLOT, CELLS)
    out_sums[0] = depth_sums(w_out, fields, 1, 1)
    exchange(0, out_sums, 0, down)
    out_sums[1] = depth_sums(w_out, fields, 1, -1)
    exchange(1, out_sums, 1, up)

    to_sibling(grads, 0, 0, fgs, fgr).wait_recv()
    pass_on(grads, FIRST + SECOND, g_sems)
    grad_fields = grads[...].reshape(CHAN * SLOT, CELLS)
    in_sums[0] = depth_sums(w_in, grad_fields, -1, 1)
    exchange(2, in_sums, 0, up)
    in_sums[1] = depth_sums(w_in, grad_fields, -1, -1)
    exchange(3, in_sums, 1, down)
    pl.when(jnp.logical_not(even))(reduce_piece)
    out_sums[4] = depth_sums(w_out, fields, 1, 0)
    in_sums[4] = depth_sums(w_in, grad_fields, -1, 0)

    row = iota((9 * 32, 256), 0)
    main_rows = onehot(
        ((row >> 5) * TAPS + (row & 31) == iota((9 * 32, 256), 1)) & ((row & 31) < TAPS)
    )
    row = iota((3 * 32, 256), 0)
    side_at = (row >> 5) * TAPS + (row & 31)
    side_rows = [
        onehot((side_at + SIDE * j == iota((3 * 32, 256), 1)) & ((row & 31) < TAPS))
        for j in range(3)
    ]

    def lanes(half, index):
        slot = divide(index, BLOCK, 96)
        to_x = (x_at + 2 * half + (slot >> 2)) & 3
        to_z = (z_lo + (slot >> 1)) & 1
        to_core = (core + slot) & 1
        return (to_x * 4 + to_z * 2 + to_core) * BLOCK + index - slot * BLOCK

    lane = iota((128, 1), 0)
    target = iota((128, C), 1)
    main_lanes = [onehot((lanes(h, lane) == target) & (lane < 96)) for h in range(2)]
    side_lanes = [
        [onehot((lanes(h, jnp.maximum(lane - 96, 0) + 32 * j) == target) & (lane >= 96))
         for j in range(3)]
        for h in range(2)
    ]

    for slot, buf in ((0, out_sums), (1, out_sums), (2, in_sums), (3, in_sums)):
        side = slot % 2
        send(buf.at[side], buf.at[side + 2], xs.at[slot], xr.at[slot], {"space": up}).wait_recv()
    conv_ref[...] = (out_sums[4] + out_sums[2] + out_sums[3])[:BLOCK].astype(BF16)
    gin_ref[...] = (in_sums[4] + in_sums[2] + in_sums[3])[:BLOCK].astype(BF16)

    send(final.at[bulk], final.at[bulk], as_, ar, {"space": up}).wait_recv()
    main = jnp.zeros((9 * 32, C), F32)
    side = jnp.zeros((3 * 32, C), F32)
    for h in range(2):
        table = final[16 * h : 16 * h + 16].reshape(256, 128)
        main = main + dot(dot(main_rows, table).astype(BF16), main_lanes[h])
        for j in range(3):
            side = side + dot(dot(side_rows[j], table).astype(BF16), side_lanes[h][j])
    gw_ref[0:9] = main.astype(BF16).reshape(9, 32, C)[:, :TAPS, :]
    gw_ref[9:12] = side.astype(BF16).reshape(3, 32, C)[:, :TAPS, :]

    for copy in started:
        copy.wait_send()
    send(got.at[bulk], got.at[bulk], rs, rr, {"space": up}).wait_send()
    send(final.at[bulk], final.at[bulk], as_, ar, {"space": up}).wait_send()


def store(conv_ref, gin_ref, gw_ref, conv_out, gin_out, gw_out, sems):
    copies = [
        pltpu.make_async_copy(src, dst, sems.at[i])
        for i, (src, dst) in enumerate(
            ((gw_ref, gw_out), (conv_ref, conv_out), (gin_ref, gin_out))
        )
    ]
    for copy in copies:
        copy.start()
    for copy in copies:
        copy.wait()


def on_device(volume, weights, grad_out):
    vmem = pl.BlockSpec(memory_space=pltpu.VMEM)
    hbm = pl.BlockSpec(memory_space=pltpu.HBM)
    dma = pltpu.SemaphoreType.DMA
    conv, gin, gw = pl.pallas_call(
        kernel,
        out_shape=(
            jax.ShapeDtypeStruct((BLOCK, CELLS), BF16),
            jax.ShapeDtypeStruct((BLOCK, CELLS), BF16),
            jax.ShapeDtypeStruct((BLOCK, TAPS, C), BF16),
        ),
        in_specs=[hbm, hbm, hbm],
        out_specs=(vmem, vmem, vmem),
        scratch_shapes=[
            pltpu.VMEM((BLOCK, CELLS), BF16),
            pltpu.VMEM((BLOCK, CELLS), BF16),
            pltpu.VMEM((CHAN, SLOT, CELLS), BF16),
            pltpu.VMEM((CHAN, SLOT, CELLS), BF16),
            pltpu.VMEM((2, SLOT, CELLS), BF16),
            pltpu.VMEM((TAPS, C, C), BF16),
            pltpu.VMEM((TAPS * SLOT, CHAN * SLOT), BF16),
            pltpu.VMEM((TAPS * SLOT, CHAN * SLOT), BF16),
            pltpu.VMEM((TAPS * SLOT, CELLS), BF16),
            pltpu.VMEM((5, SLOT, CELLS), F32),
            pltpu.VMEM((5, SLOT, CELLS), F32),
            pltpu.VMEM((MEMBERS, 16, 128), F32),
            pltpu.VMEM((MEMBERS, 16, 128), F32),
            pltpu.VMEM((MEMBERS, 16, 128), BF16),
            dma((3,)),
            dma((8,)), dma((8,)), dma((8,)), dma((8,)),
            dma((8,)), dma((8,)), dma((8,)), dma((8,)),
            dma((2,)), dma((2,)), dma((4,)), dma((4,)),
            dma, dma, dma, dma,
        ],
        compiler_params=pltpu.CompilerParams(
            collective_id=0, has_side_effects=True, vmem_limit_bytes=54000 * 1024
        ),
        cost_estimate=pl.CostEstimate(
            flops=400_000_000, bytes_accessed=3_000_000, transcendentals=0
        ),
    )(*(pltpu.with_memory_space_constraint(a, pltpu.HBM) for a in
        (volume.reshape(BLOCK, CELLS), weights, grad_out.reshape(BLOCK, CELLS))))
    conv, gin, gw = pl.pallas_call(
        store,
        out_shape=tuple(jax.ShapeDtypeStruct(a.shape, a.dtype) for a in (conv, gin, gw)),
        in_specs=[vmem, vmem, vmem],
        out_specs=(hbm, hbm, hbm),
        scratch_shapes=[dma((3,))],
    )(*(pltpu.with_memory_space_constraint(a, pltpu.VMEM) for a in (conv, gin, gw)))
    shape = volume.shape
    return conv.reshape(shape), gin.reshape(shape), jnp.transpose(gw, (1, 2, 0))


def solution(mesh):
    return jax.shard_map(
        on_device,
        mesh=mesh,
        in_specs=(P("rep", "chan", "space", None), P(), P("rep", "chan", "space", None)),
        out_specs=(
            P("rep", "chan", "space", None),
            P("rep", "chan", "space", None),
            P(None, None, "chan"),
        ),
        check_vma=False,
    )
```

```python
import math

import jax
import jax.numpy as jnp
from jax import lax
from jax.experimental import pallas as pl
from jax.experimental.pallas import tpu as pltpu
from jax.sharding import PartitionSpec as P

H = 32
W = 32
CELLS = H * W
C = 192
BLOCK = 12
SLOT = 16
CHAN = 16
SPACE = 8
REP = 4
TAPS = 27
MEMBERS = SPACE * REP
MAIN = 243
SIDE = 81
FACTOR = 1.0 / math.sqrt(4 * 8 * 1024)
MESH = pl.DeviceIdType.MESH
F32 = jnp.float32
BF16 = jnp.bfloat16
FIRST = ((0, 1), (1, 0), (1, 1))
SECOND = ((3, 0), (3, 1), (2, 0), (2, 1))

FAR_FIRST = sorted(
    ((dy, dz) for dz in (2, 1, 3, 0) for dy in (4, 3, 5, 2, 6, 1, 7, 0) if dy or dz),
    key=lambda at: -(min(at[0], 8 - at[0]) + 2 * min(at[1], 4 - at[1])),
)


def onehot(cond):
    return jnp.where(cond, 1.0, 0.0).astype(BF16)


def iota(shape, dim):
    return lax.broadcasted_iota(jnp.int32, shape, dim)


def dot(a, b):
    return jnp.dot(a, b, preferred_element_type=F32)


def dot_nt(a, b):
    return lax.dot_general(a, b, (((1,), (1,)), ((), ())), preferred_element_type=F32)


def shift_cols(x, by):
    if by == 0:
        return x
    col = iota(x.shape, 1) & (W - 1)
    if by > 0:
        return jnp.where(col == W - 1, pltpu.roll(x, W - 1, 1), pltpu.roll(x, CELLS - 1, 1))
    return jnp.where(col == 0, pltpu.roll(x, CELLS - (W - 1), 1), pltpu.roll(x, 1, 1))


def shift_rows(x, by):
    if by == 0:
        return x
    return pltpu.roll(x, (-by * W) % CELLS, 1)


def depth_sums(rows, fields, sign, depth_off):
    first = (depth_off + 1) * 9 * SLOT
    products = dot(rows[first : first + 9 * SLOT, :], fields)
    total = None
    for row_off in (-1, 0, 1):
        line = None
        for col_off in (-1, 0, 1):
            at = ((row_off + 1) * 3 + col_off + 1) * SLOT
            term = shift_cols(products[at : at + SLOT], sign * col_off)
            line = term if line is None else line + term
        line = shift_rows(line, sign * row_off)
        total = line if total is None else total + line
    return total


def divide(x, by, below):
    out = jnp.zeros_like(x)
    for k in range(by, below, by):
        out = out + jnp.where(x >= k, 1, 0)
    return out


def kernel(
    vol_ref, w_ref, grad_ref,
    conv_ref, gin_ref, gw_ref,
    vol_in, grad_in, vols, grads, halo, w_vmem, w_out, w_in, cols, out_sums, in_sums,
    parts, got, final,
    in_sem, vs, vr, gs, gr, fvs, fvr, fgs, fgr, hs, hr, xs, xr, rs, rr, as_, ar,
):
    space = lax.axis_index("space")
    chan = lax.axis_index("chan")
    rep = lax.axis_index("rep")
    core = chan & 1
    z_lo = (chan >> 1) & 1
    x_at = chan >> 2
    sibling = chan + 1 - 2 * core
    up = (space + 1) & 7
    down = (space + 7) & 7
    me = space * REP + rep

    vol_copy = pltpu.make_async_copy(vol_ref, vol_in, in_sem.at[0])
    grad_copy = pltpu.make_async_copy(grad_ref, grad_in, in_sem.at[1])
    w_copy = pltpu.make_async_copy(w_ref, w_vmem, in_sem.at[2])
    vol_copy.start()
    grad_copy.start()
    w_copy.start()

    def chip_at(dx, dz):
        return ((x_at + dx) & 3) * 4 + ((z_lo + dz) & 1) * 2 + core

    barrier = pltpu.get_barrier_semaphore()
    for dx, dz in FIRST + SECOND:
        pl.semaphore_signal(barrier, inc=1, device_id={"chan": chip_at(dx, dz)}, device_id_type=MESH)
    pl.semaphore_signal(barrier, inc=1, device_id={"chan": sibling}, device_id_type=MESH)
    for dz in range(2):
        pl.semaphore_signal(
            barrier, inc=1, device_id={"chan": chip_at(2, dz) ^ 1}, device_id_type=MESH
        )
    for dy, dz in FAR_FIRST:
        pl.semaphore_signal(
            barrier, inc=1, device_id={"space": (space + dy) & 7, "rep": (rep + dz) & 3},
            device_id_type=MESH,
        )

    pad = jnp.zeros((SLOT - BLOCK, CELLS), F32)
    vol_copy.wait()
    vols[0] = jnp.concatenate([vol_in[...].astype(F32), pad], axis=0).astype(BF16)
    grad_copy.wait()
    own_grad = jnp.concatenate([grad_in[...].astype(F32), pad], axis=0)
    grads[0] = own_grad.astype(BF16)
    pl.semaphore_wait(barrier, 7 + 1 + 2 + MEMBERS - 1)

    def send(src, dst, s_sem, r_sem, where):
        return pltpu.make_async_remote_copy(
            src_ref=src, dst_ref=dst, send_sem=s_sem, recv_sem=r_sem,
            device_id=where, device_id_type=MESH,
        )

    def to_peer(buf, dx, dz, s_sem, r_sem):
        slot = dx * 4 + dz * 2
        return send(buf.at[0], buf.at[slot], s_sem.at[slot // 2], r_sem.at[slot // 2],
                    {"chan": chip_at(4 - dx, dz)})

    def to_sibling(buf, dx, dz, s_sem, r_sem):
        slot = dx * 4 + dz * 2
        return send(buf.at[slot], buf.at[slot + 1], s_sem.at[slot // 2], r_sem.at[slot // 2],
                    {"chan": sibling})

    def to_far_core(buf, dx, dz, s_sem, r_sem):
        slot = dx * 4 + dz * 2
        return send(buf.at[0], buf.at[slot + 1], s_sem.at[slot // 2], r_sem.at[slot // 2],
                    {"chan": chip_at(4 - dx, dz) ^ 1})

    started = []

    def go(copy):
        copy.start()
        started.append(copy)

    def pass_on(buf, group, sems, direct=False):
        s_sem, r_sem, fs_sem, fr_sem = sems
        for dx, dz in group:
            to_peer(buf, dx, dz, s_sem, r_sem).wait_recv()
            if not (direct and dx == 2):
                go(to_sibling(buf, dx, dz, fs_sem, fr_sem))
        for dx, dz in group:
            to_sibling(buf, dx, dz, fs_sem, fr_sem).wait_recv()

    v_sems = (vs, vr, fvs, fvr)
    g_sems = (gs, gr, fgs, fgr)
    for dx, dz in FIRST:
        go(to_peer(vols, dx, dz, vs, vr))
    go(to_sibling(vols, 0, 0, fvs, fvr))
    halo_up = send(grads.at[0], halo.at[0], hs.at[0], hr.at[0], {"space": up})
    halo_down = send(grads.at[0], halo.at[1], hs.at[1], hr.at[1], {"space": down})
    go(halo_up)
    go(halo_down)
    for dx, dz in SECOND:
        go(to_peer(vols, dx, dz, vs, vr))
        if dx == 2:
            go(to_far_core(vols, dx, dz, fvs, fvr))
    for dx, dz in FIRST + SECOND:
        go(to_peer(grads, dx, dz, gs, gr))
    go(to_sibling(grads, 0, 0, fgs, fgr))

    row = iota((328, TAPS * SLOT), 0)
    col = iota((328, TAPS * SLOT), 1)
    order = onehot(((col & 15) * TAPS + (col >> 4) == row) & ((col & 15) < BLOCK))
    row = iota((96, 128), 0)
    col = iota((96, 128), 1)
    compact = onehot(((col >> 4) * BLOCK + (col & 15) == row) & ((col & 15) < BLOCK))

    def columns(depth_off, plane):
        for col_off in (-1, 0, 1):
            moved = shift_cols(plane, -col_off)
            for row_off in (-1, 0, 1):
                tap = (depth_off + 1) * 9 + (row_off + 1) * 3 + col_off + 1
                cols[tap * SLOT : (tap + 1) * SLOT, :] = shift_rows(moved, -row_off).astype(BF16)

    columns(0, own_grad)
    halo_up.wait_recv()
    columns(1, halo[0].astype(F32))
    halo_down.wait_recv()
    columns(-1, halo[1].astype(F32))
    ordered = dot(order, cols[...]).astype(BF16)

    def scatter(half):
        fields = vols[8 * half : 8 * half + 8].reshape(8 * SLOT, CELLS)
        packed = dot(compact, fields).astype(BF16)
        sums = dot_nt(ordered, packed)
        side = sums[MAIN : MAIN + SIDE]
        side = jnp.concatenate(
            [side[:, 0:32], side[:, 32:64], side[:, 64:96], jnp.zeros((13, 32), F32)], axis=0
        )
        parts[16 * half : 16 * half + 16] = jnp.concatenate([sums[:256], side], axis=1).reshape(
            16, 16, 128
        )
        for dz in (2, 1, 3, 0):
            for k in (2, 1, 3, 0):
                pair = ((space >> 1) + k) & 3
                y, z = 2 * pair + half, (rep + dz) & 3
                copy = send(parts.at[16 * half + pair * REP + z], got.at[me], rs, rr,
                            {"space": y, "rep": z})
                if k == 0 and dz == 0:
                    pl.when(y != space)(copy.start)
                else:
                    copy.start()

    to_sibling(vols, 0, 0, fvs, fvr).wait_recv()
    pass_on(vols, FIRST, v_sems)
    scatter(0)
    lane = iota((C, CHAN * SLOT), 1)
    at_x = (x_at + (lane >> 6)) & 3
    at_z = (z_lo + (lane >> 5)) & 1
    at_core = (core + (lane >> 4)) & 1
    block = (at_x * 4 + at_z * 2 + at_core) * BLOCK
    slot_of = onehot((block + (lane & 15) == iota((C, CHAN * SLOT), 0)) & ((lane & 15) < BLOCK))
    row = iota((SLOT, C), 0)
    mine = onehot((iota((SLOT, C), 1) == chan * BLOCK + row) & (row < BLOCK))
    w_copy.wait()
    picked = [dot_nt(mine, w_vmem[tap]).astype(BF16) for tap in range(TAPS)]
    w_out[...] = dot(jnp.concatenate(picked, axis=0), slot_of).astype(BF16)
    pass_on(vols, SECOND, v_sems, direct=True)
    scatter(1)
    picked = [dot(mine, w_vmem[tap]).astype(BF16) for tap in range(TAPS)]
    w_in[...] = dot(jnp.concatenate(picked, axis=0), slot_of).astype(BF16)

    own_four = (space & 1) * 16 + (space >> 1) * REP
    piece = own_four + rep
    bulk = pl.ds(0, MEMBERS - 1)

    def reduce_piece():
        got[me] = parts[piece]
        send(got.at[bulk], got.at[bulk], rs, rr, {"space": up}).wait_recv()
        final[piece] = (jnp.sum(got[...], axis=0) * FACTOR).astype(BF16)
        for dy, dz in FAR_FIRST:
            send(final.at[piece], final.at[piece], as_, ar, {
                "space": (space + dy) & 7, "rep": (rep + dz) & 3
            }).start()

    even = (space & 1) == 0


    def exchange(slot, buf, side_at, where):
        go(send(buf.at[side_at], buf.at[side_at + 2], xs.at[slot], xr.at[slot], {"space": where}))

    fields = vols[...].reshape(CHAN * SLOT, CELLS)
    out_sums[0] = depth_sums(w_out, fields, 1, 1)
    exchange(0, out_sums, 0, down)
    out_sums[1] = depth_sums(w_out, fields, 1, -1)
    exchange(1, out_sums, 1, up)

    to_sibling(grads, 0, 0, fgs, fgr).wait_recv()
    pass_on(grads, FIRST + SECOND, g_sems)
    grad_fields = grads[...].reshape(CHAN * SLOT, CELLS)
    in_sums[0] = depth_sums(w_in, grad_fields, -1, 1)
    exchange(2, in_sums, 0, up)
    in_sums[1] = depth_sums(w_in, grad_fields, -1, -1)
    exchange(3, in_sums, 1, down)
    reduce_piece()
    out_sums[4] = depth_sums(w_out, fields, 1, 0)
    in_sums[4] = depth_sums(w_in, grad_fields, -1, 0)

    row = iota((9 * 32, 256), 0)
    main_rows = onehot(
        ((row >> 5) * TAPS + (row & 31) == iota((9 * 32, 256), 1)) & ((row & 31) < TAPS)
    )
    row = iota((3 * 32, 256), 0)
    side_at = (row >> 5) * TAPS + (row & 31)
    side_rows = [
        onehot((side_at + SIDE * j == iota((3 * 32, 256), 1)) & ((row & 31) < TAPS))
        for j in range(3)
    ]

    def lanes(half, index):
        slot = divide(index, BLOCK, 96)
        to_x = (x_at + 2 * half + (slot >> 2)) & 3
        to_z = (z_lo + (slot >> 1)) & 1
        to_core = (core + slot) & 1
        return (to_x * 4 + to_z * 2 + to_core) * BLOCK + index - slot * BLOCK

    lane = iota((128, 1), 0)
    target = iota((128, C), 1)
    main_lanes = [onehot((lanes(h, lane) == target) & (lane < 96)) for h in range(2)]
    side_lanes = [
        [onehot((lanes(h, jnp.maximum(lane - 96, 0) + 32 * j) == target) & (lane >= 96))
         for j in range(3)]
        for h in range(2)
    ]

    for slot, buf in ((0, out_sums), (1, out_sums), (2, in_sums), (3, in_sums)):
        side = slot % 2
        send(buf.at[side], buf.at[side + 2], xs.at[slot], xr.at[slot], {"space": up}).wait_recv()
    conv_ref[...] = (out_sums[4] + out_sums[2] + out_sums[3])[:BLOCK].astype(BF16)
    gin_ref[...] = (in_sums[4] + in_sums[2] + in_sums[3])[:BLOCK].astype(BF16)

    send(final.at[bulk], final.at[bulk], as_, ar, {"space": up}).wait_recv()
    main = jnp.zeros((9 * 32, C), F32)
    side = jnp.zeros((3 * 32, C), F32)
    for h in range(2):
        table = final[16 * h : 16 * h + 16].reshape(256, 128)
        main = main + dot(dot(main_rows, table).astype(BF16), main_lanes[h])
        for j in range(3):
            side = side + dot(dot(side_rows[j], table).astype(BF16), side_lanes[h][j])
    gw_ref[0:9] = main.astype(BF16).reshape(9, 32, C)[:, :TAPS, :]
    gw_ref[9:12] = side.astype(BF16).reshape(3, 32, C)[:, :TAPS, :]

    for copy in started:
        copy.wait_send()
    send(got.at[bulk], got.at[bulk], rs, rr, {"space": up}).wait_send()
    send(final.at[bulk], final.at[bulk], as_, ar, {"space": up}).wait_send()


def store(conv_ref, gin_ref, gw_ref, conv_out, gin_out, gw_out, sems):
    copies = [
        pltpu.make_async_copy(src, dst, sems.at[i])
        for i, (src, dst) in enumerate(
            ((gw_ref, gw_out), (conv_ref, conv_out), (gin_ref, gin_out))
        )
    ]
    for copy in copies:
        copy.start()
    for copy in copies:
        copy.wait()


def on_device(volume, weights, grad_out):
    vmem = pl.BlockSpec(memory_space=pltpu.VMEM)
    hbm = pl.BlockSpec(memory_space=pltpu.HBM)
    dma = pltpu.SemaphoreType.DMA
    conv, gin, gw = pl.pallas_call(
        kernel,
        out_shape=(
            jax.ShapeDtypeStruct((BLOCK, CELLS), BF16),
            jax.ShapeDtypeStruct((BLOCK, CELLS), BF16),
            jax.ShapeDtypeStruct((BLOCK, TAPS, C), BF16),
        ),
        in_specs=[hbm, hbm, hbm],
        out_specs=(vmem, vmem, vmem),
        scratch_shapes=[
            pltpu.VMEM((BLOCK, CELLS), BF16),
            pltpu.VMEM((BLOCK, CELLS), BF16),
            pltpu.VMEM((CHAN, SLOT, CELLS), BF16),
            pltpu.VMEM((CHAN, SLOT, CELLS), BF16),
            pltpu.VMEM((2, SLOT, CELLS), BF16),
            pltpu.VMEM((TAPS, C, C), BF16),
            pltpu.VMEM((TAPS * SLOT, CHAN * SLOT), BF16),
            pltpu.VMEM((TAPS * SLOT, CHAN * SLOT), BF16),
            pltpu.VMEM((TAPS * SLOT, CELLS), BF16),
            pltpu.VMEM((5, SLOT, CELLS), F32),
            pltpu.VMEM((5, SLOT, CELLS), F32),
            pltpu.VMEM((MEMBERS, 16, 128), F32),
            pltpu.VMEM((MEMBERS, 16, 128), F32),
            pltpu.VMEM((MEMBERS, 16, 128), BF16),
            dma((3,)),
            dma((8,)), dma((8,)), dma((8,)), dma((8,)),
            dma((8,)), dma((8,)), dma((8,)), dma((8,)),
            dma((2,)), dma((2,)), dma((4,)), dma((4,)),
            dma, dma, dma, dma,
        ],
        compiler_params=pltpu.CompilerParams(
            collective_id=0, has_side_effects=True, vmem_limit_bytes=54000 * 1024
        ),
        cost_estimate=pl.CostEstimate(
            flops=400_000_000, bytes_accessed=3_000_000, transcendentals=0
        ),
    )(*(pltpu.with_memory_space_constraint(a, pltpu.HBM) for a in
        (volume.reshape(BLOCK, CELLS), weights, grad_out.reshape(BLOCK, CELLS))))
    conv, gin, gw = pl.pallas_call(
        store,
        out_shape=tuple(jax.ShapeDtypeStruct(a.shape, a.dtype) for a in (conv, gin, gw)),
        in_specs=[vmem, vmem, vmem],
        out_specs=(hbm, hbm, hbm),
        scratch_shapes=[dma((3,))],
    )(*(pltpu.with_memory_space_constraint(a, pltpu.VMEM) for a in (conv, gin, gw)))
    shape = volume.shape
    return conv.reshape(shape), gin.reshape(shape), jnp.transpose(gw, (1, 2, 0))


def solution(mesh):
    return jax.shard_map(
        on_device,
        mesh=mesh,
        in_specs=(P("rep", "chan", "space", None), P(), P("rep", "chan", "space", None)),
        out_specs=(
            P("rep", "chan", "space", None),
            P("rep", "chan", "space", None),
            P(None, None, "chan"),
        ),
        check_vma=False,
    )
```

```python
import math

import jax
import jax.numpy as jnp
from jax import lax
from jax.experimental import pallas as pl
from jax.experimental.pallas import tpu as pltpu
from jax.sharding import PartitionSpec as P

H = 32
W = 32
CELLS = H * W
C = 192
BLOCK = 12
SLOT = 16
CHAN = 16
SPACE = 8
REP = 4
TAPS = 27
MEMBERS = SPACE * REP
MAIN = 243
SIDE = 81
FACTOR = 1.0 / math.sqrt(4 * 8 * 1024)
MESH = pl.DeviceIdType.MESH
F32 = jnp.float32
BF16 = jnp.bfloat16
FIRST = ((0, 1), (1, 0), (1, 1))
SECOND = ((3, 0), (3, 1), (2, 0), (2, 1))

FAR_FIRST = sorted(
    ((dy, dz) for dz in (2, 1, 3, 0) for dy in (4, 3, 5, 2, 6, 1, 7, 0) if dy or dz),
    key=lambda at: -(min(at[0], 8 - at[0]) + 2 * min(at[1], 4 - at[1])),
)


def onehot(cond):
    return jnp.where(cond, 1.0, 0.0).astype(BF16)


def iota(shape, dim):
    return lax.broadcasted_iota(jnp.int32, shape, dim)


def dot(a, b):
    return jnp.dot(a, b, preferred_element_type=F32)


def dot_nt(a, b):
    return lax.dot_general(a, b, (((1,), (1,)), ((), ())), preferred_element_type=F32)


def shift_cols(x, by):
    if by == 0:
        return x
    col = iota(x.shape, 1) & (W - 1)
    if by > 0:
        return jnp.where(col == W - 1, pltpu.roll(x, W - 1, 1), pltpu.roll(x, CELLS - 1, 1))
    return jnp.where(col == 0, pltpu.roll(x, CELLS - (W - 1), 1), pltpu.roll(x, 1, 1))


def shift_rows(x, by):
    if by == 0:
        return x
    return pltpu.roll(x, (-by * W) % CELLS, 1)


def depth_sums(rows, fields, sign, depth_off):
    first = (depth_off + 1) * 9 * SLOT
    products = dot(rows[first : first + 9 * SLOT, :], fields)
    total = None
    for row_off in (-1, 0, 1):
        line = None
        for col_off in (-1, 0, 1):
            at = ((row_off + 1) * 3 + col_off + 1) * SLOT
            term = shift_cols(products[at : at + SLOT], sign * col_off)
            line = term if line is None else line + term
        line = shift_rows(line, sign * row_off)
        total = line if total is None else total + line
    return total


def divide(x, by, below):
    out = jnp.zeros_like(x)
    for k in range(by, below, by):
        out = out + jnp.where(x >= k, 1, 0)
    return out


def kernel(
    vol_ref, w_ref, grad_ref,
    conv_ref, gin_ref, gw_ref,
    vol_in, grad_in, vols, grads, halo, w_vmem, w_out, w_in, cols, out_sums, in_sums,
    parts, got, final,
    in_sem, vs, vr, gs, gr, fvs, fvr, fgs, fgr, hs, hr, xs, xr, rs, rr, as_, ar,
):
    space = lax.axis_index("space")
    chan = lax.axis_index("chan")
    rep = lax.axis_index("rep")
    core = chan & 1
    z_lo = (chan >> 1) & 1
    x_at = chan >> 2
    sibling = chan + 1 - 2 * core
    up = (space + 1) & 7
    down = (space + 7) & 7
    me = space * REP + rep

    vol_copy = pltpu.make_async_copy(vol_ref, vol_in, in_sem.at[0])
    grad_copy = pltpu.make_async_copy(grad_ref, grad_in, in_sem.at[1])
    w_copy = pltpu.make_async_copy(w_ref, w_vmem, in_sem.at[2])
    vol_copy.start()
    grad_copy.start()
    w_copy.start()

    def chip_at(dx, dz):
        return ((x_at + dx) & 3) * 4 + ((z_lo + dz) & 1) * 2 + core

    barrier = pltpu.get_barrier_semaphore()
    for dx, dz in FIRST + SECOND:
        pl.semaphore_signal(barrier, inc=1, device_id={"chan": chip_at(dx, dz)}, device_id_type=MESH)
    pl.semaphore_signal(barrier, inc=1, device_id={"chan": sibling}, device_id_type=MESH)
    for dz in range(2):
        pl.semaphore_signal(
            barrier, inc=1, device_id={"chan": chip_at(2, dz) ^ 1}, device_id_type=MESH
        )
    for dy, dz in FAR_FIRST:
        pl.semaphore_signal(
            barrier, inc=1, device_id={"space": (space + dy) & 7, "rep": (rep + dz) & 3},
            device_id_type=MESH,
        )

    pad = jnp.zeros((SLOT - BLOCK, CELLS), F32)
    vol_copy.wait()
    vols[0] = jnp.concatenate([vol_in[...].astype(F32), pad], axis=0).astype(BF16)
    grad_copy.wait()
    own_grad = jnp.concatenate([grad_in[...].astype(F32), pad], axis=0)
    grads[0] = own_grad.astype(BF16)
    pl.semaphore_wait(barrier, 7 + 1 + 2 + MEMBERS - 1)

    def send(src, dst, s_sem, r_sem, where):
        return pltpu.make_async_remote_copy(
            src_ref=src, dst_ref=dst, send_sem=s_sem, recv_sem=r_sem,
            device_id=where, device_id_type=MESH,
        )

    def to_peer(buf, dx, dz, s_sem, r_sem):
        slot = dx * 4 + dz * 2
        return send(buf.at[0], buf.at[slot], s_sem.at[slot // 2], r_sem.at[slot // 2],
                    {"chan": chip_at(4 - dx, dz)})

    def to_sibling(buf, dx, dz, s_sem, r_sem):
        slot = dx * 4 + dz * 2
        return send(buf.at[slot], buf.at[slot + 1], s_sem.at[slot // 2], r_sem.at[slot // 2],
                    {"chan": sibling})

    def to_far_core(buf, dx, dz, s_sem, r_sem):
        slot = dx * 4 + dz * 2
        return send(buf.at[0], buf.at[slot + 1], s_sem.at[slot // 2], r_sem.at[slot // 2],
                    {"chan": chip_at(4 - dx, dz) ^ 1})

    started = []

    def go(copy):
        copy.start()
        started.append(copy)

    def pass_on(buf, group, sems, direct=False):
        s_sem, r_sem, fs_sem, fr_sem = sems
        for dx, dz in group:
            to_peer(buf, dx, dz, s_sem, r_sem).wait_recv()
            if not (direct and dx == 2):
                go(to_sibling(buf, dx, dz, fs_sem, fr_sem))
        for dx, dz in group:
            to_sibling(buf, dx, dz, fs_sem, fr_sem).wait_recv()

    v_sems = (vs, vr, fvs, fvr)
    g_sems = (gs, gr, fgs, fgr)
    for dx, dz in FIRST:
        go(to_peer(vols, dx, dz, vs, vr))
    go(to_sibling(vols, 0, 0, fvs, fvr))
    halo_up = send(grads.at[0], halo.at[0], hs.at[0], hr.at[0], {"space": up})
    halo_down = send(grads.at[0], halo.at[1], hs.at[1], hr.at[1], {"space": down})
    go(halo_up)
    go(halo_down)
    for dx, dz in SECOND:
        go(to_peer(vols, dx, dz, vs, vr))
        if dx == 2:
            go(to_far_core(vols, dx, dz, fvs, fvr))
    for dx, dz in FIRST + SECOND:
        go(to_peer(grads, dx, dz, gs, gr))
    go(to_sibling(grads, 0, 0, fgs, fgr))

    row = iota((328, TAPS * SLOT), 0)
    col = iota((328, TAPS * SLOT), 1)
    order = onehot(((col & 15) * TAPS + (col >> 4) == row) & ((col & 15) < BLOCK))
    row = iota((96, 128), 0)
    col = iota((96, 128), 1)
    compact = onehot(((col >> 4) * BLOCK + (col & 15) == row) & ((col & 15) < BLOCK))

    def columns(depth_off, plane):
        for col_off in (-1, 0, 1):
            moved = shift_cols(plane, -col_off)
            for row_off in (-1, 0, 1):
                tap = (depth_off + 1) * 9 + (row_off + 1) * 3 + col_off + 1
                cols[tap * SLOT : (tap + 1) * SLOT, :] = shift_rows(moved, -row_off).astype(BF16)

    columns(0, own_grad)
    halo_up.wait_recv()
    columns(1, halo[0].astype(F32))
    halo_down.wait_recv()
    columns(-1, halo[1].astype(F32))
    ordered = dot(order, cols[...]).astype(BF16)

    def scatter(half):
        fields = vols[8 * half : 8 * half + 8].reshape(8 * SLOT, CELLS)
        packed = dot(compact, fields).astype(BF16)
        sums = dot_nt(ordered, packed)
        side = sums[MAIN : MAIN + SIDE]
        side = jnp.concatenate(
            [side[:, 0:32], side[:, 32:64], side[:, 64:96], jnp.zeros((13, 32), F32)], axis=0
        )
        parts[16 * half : 16 * half + 16] = jnp.concatenate([sums[:256], side], axis=1).reshape(
            16, 16, 128
        )
        for dz in (2, 1, 3, 0):
            for k in (2, 1, 3, 0):
                pair = ((space >> 1) + k) & 3
                y, z = 2 * pair + half, (rep + dz) & 3
                copy = send(parts.at[16 * half + pair * REP + z], got.at[me], rs, rr,
                            {"space": y, "rep": z})
                if k == 0 and dz == 0:
                    pl.when(y != space)(copy.start)
                else:
                    copy.start()

    to_sibling(vols, 0, 0, fvs, fvr).wait_recv()
    pass_on(vols, FIRST, v_sems)
    scatter(0)
    lane = iota((C, CHAN * SLOT), 1)
    at_x = (x_at + (lane >> 6)) & 3
    at_z = (z_lo + (lane >> 5)) & 1
    at_core = (core + (lane >> 4)) & 1
    block = (at_x * 4 + at_z * 2 + at_core) * BLOCK
    slot_of = onehot((block + (lane & 15) == iota((C, CHAN * SLOT), 0)) & ((lane & 15) < BLOCK))
    row = iota((SLOT, C), 0)
    mine = onehot((iota((SLOT, C), 1) == chan * BLOCK + row) & (row < BLOCK))
    w_copy.wait()
    picked = [dot_nt(mine, w_vmem[tap]).astype(BF16) for tap in range(TAPS)]
    w_out[...] = dot(jnp.concatenate(picked, axis=0), slot_of).astype(BF16)
    pass_on(vols, SECOND, v_sems, direct=True)
    scatter(1)
    picked = [dot(mine, w_vmem[tap]).astype(BF16) for tap in range(TAPS)]
    w_in[...] = dot(jnp.concatenate(picked, axis=0), slot_of).astype(BF16)

    own_four = (space & 1) * 16 + (space >> 1) * REP
    piece = own_four + rep
    bulk = pl.ds(0, MEMBERS - 1)

    def reduce_piece():
        got[me] = parts[piece]
        send(got.at[bulk], got.at[bulk], rs, rr, {"space": up}).wait_recv()
        final[piece] = (jnp.sum(got[...], axis=0) * FACTOR).astype(BF16)
        for dy, dz in FAR_FIRST:
            send(final.at[piece], final.at[piece], as_, ar, {
                "space": (space + dy) & 7, "rep": (rep + dz) & 3
            }).start()

    even = (space & 1) == 0


    def exchange(slot, buf, side_at, where):
        go(send(buf.at[side_at], buf.at[side_at + 2], xs.at[slot], xr.at[slot], {"space": where}))

    fields = vols[...].reshape(CHAN * SLOT, CELLS)
    out_sums[0] = depth_sums(w_out, fields, 1, 1)
    exchange(0, out_sums, 0, down)
    out_sums[1] = depth_sums(w_out, fields, 1, -1)
    exchange(1, out_sums, 1, up)

    for dx, dz in FIRST:
        to_peer(grads, dx, dz, gs, gr).wait_recv()
        go(to_sibling(grads, dx, dz, fgs, fgr))
    for dx, dz in SECOND:
        to_peer(grads, dx, dz, gs, gr).wait_recv()
        go(to_sibling(grads, dx, dz, fgs, fgr))
    reduce_piece()
    to_sibling(grads, 0, 0, fgs, fgr).wait_recv()
    for dx, dz in FIRST + SECOND:
        to_sibling(grads, dx, dz, fgs, fgr).wait_recv()
    grad_fields = grads[...].reshape(CHAN * SLOT, CELLS)
    in_sums[0] = depth_sums(w_in, grad_fields, -1, 1)
    exchange(2, in_sums, 0, up)
    in_sums[1] = depth_sums(w_in, grad_fields, -1, -1)
    exchange(3, in_sums, 1, down)
    out_sums[4] = depth_sums(w_out, fields, 1, 0)
    in_sums[4] = depth_sums(w_in, grad_fields, -1, 0)

    row = iota((9 * 32, 256), 0)
    main_rows = onehot(
        ((row >> 5) * TAPS + (row & 31) == iota((9 * 32, 256), 1)) & ((row & 31) < TAPS)
    )
    row = iota((3 * 32, 256), 0)
    side_at = (row >> 5) * TAPS + (row & 31)
    side_rows = [
        onehot((side_at + SIDE * j == iota((3 * 32, 256), 1)) & ((row & 31) < TAPS))
        for j in range(3)
    ]

    def lanes(half, index):
        slot = divide(index, BLOCK, 96)
        to_x = (x_at + 2 * half + (slot >> 2)) & 3
        to_z = (z_lo + (slot >> 1)) & 1
        to_core = (core + slot) & 1
        return (to_x * 4 + to_z * 2 + to_core) * BLOCK + index - slot * BLOCK

    lane = iota((128, 1), 0)
    target = iota((128, C), 1)
    main_lanes = [onehot((lanes(h, lane) == target) & (lane < 96)) for h in range(2)]
    side_lanes = [
        [onehot((lanes(h, jnp.maximum(lane - 96, 0) + 32 * j) == target) & (lane >= 96))
         for j in range(3)]
        for h in range(2)
    ]

    for slot, buf in ((0, out_sums), (1, out_sums), (2, in_sums), (3, in_sums)):
        side = slot % 2
        send(buf.at[side], buf.at[side + 2], xs.at[slot], xr.at[slot], {"space": up}).wait_recv()
    conv_ref[...] = (out_sums[4] + out_sums[2] + out_sums[3])[:BLOCK].astype(BF16)
    gin_ref[...] = (in_sums[4] + in_sums[2] + in_sums[3])[:BLOCK].astype(BF16)

    send(final.at[bulk], final.at[bulk], as_, ar, {"space": up}).wait_recv()
    main = jnp.zeros((9 * 32, C), F32)
    side = jnp.zeros((3 * 32, C), F32)
    for h in range(2):
        table = final[16 * h : 16 * h + 16].reshape(256, 128)
        main = main + dot(dot(main_rows, table).astype(BF16), main_lanes[h])
        for j in range(3):
            side = side + dot(dot(side_rows[j], table).astype(BF16), side_lanes[h][j])
    gw_ref[0:9] = main.astype(BF16).reshape(9, 32, C)[:, :TAPS, :]
    gw_ref[9:12] = side.astype(BF16).reshape(3, 32, C)[:, :TAPS, :]

    for copy in started:
        copy.wait_send()
    send(got.at[bulk], got.at[bulk], rs, rr, {"space": up}).wait_send()
    send(final.at[bulk], final.at[bulk], as_, ar, {"space": up}).wait_send()


def store(conv_ref, gin_ref, gw_ref, conv_out, gin_out, gw_out, sems):
    copies = [
        pltpu.make_async_copy(src, dst, sems.at[i])
        for i, (src, dst) in enumerate(
            ((gw_ref, gw_out), (conv_ref, conv_out), (gin_ref, gin_out))
        )
    ]
    for copy in copies:
        copy.start()
    for copy in copies:
        copy.wait()


def on_device(volume, weights, grad_out):
    vmem = pl.BlockSpec(memory_space=pltpu.VMEM)
    hbm = pl.BlockSpec(memory_space=pltpu.HBM)
    dma = pltpu.SemaphoreType.DMA
    conv, gin, gw = pl.pallas_call(
        kernel,
        out_shape=(
            jax.ShapeDtypeStruct((BLOCK, CELLS), BF16),
            jax.ShapeDtypeStruct((BLOCK, CELLS), BF16),
            jax.ShapeDtypeStruct((BLOCK, TAPS, C), BF16),
        ),
        in_specs=[hbm, hbm, hbm],
        out_specs=(vmem, vmem, vmem),
        scratch_shapes=[
            pltpu.VMEM((BLOCK, CELLS), BF16),
            pltpu.VMEM((BLOCK, CELLS), BF16),
            pltpu.VMEM((CHAN, SLOT, CELLS), BF16),
            pltpu.VMEM((CHAN, SLOT, CELLS), BF16),
            pltpu.VMEM((2, SLOT, CELLS), BF16),
            pltpu.VMEM((TAPS, C, C), BF16),
            pltpu.VMEM((TAPS * SLOT, CHAN * SLOT), BF16),
            pltpu.VMEM((TAPS * SLOT, CHAN * SLOT), BF16),
            pltpu.VMEM((TAPS * SLOT, CELLS), BF16),
            pltpu.VMEM((5, SLOT, CELLS), F32),
            pltpu.VMEM((5, SLOT, CELLS), F32),
            pltpu.VMEM((MEMBERS, 16, 128), F32),
            pltpu.VMEM((MEMBERS, 16, 128), F32),
            pltpu.VMEM((MEMBERS, 16, 128), BF16),
            dma((3,)),
            dma((8,)), dma((8,)), dma((8,)), dma((8,)),
            dma((8,)), dma((8,)), dma((8,)), dma((8,)),
            dma((2,)), dma((2,)), dma((4,)), dma((4,)),
            dma, dma, dma, dma,
        ],
        compiler_params=pltpu.CompilerParams(
            collective_id=0, has_side_effects=True, vmem_limit_bytes=54000 * 1024
        ),
        cost_estimate=pl.CostEstimate(
            flops=400_000_000, bytes_accessed=3_000_000, transcendentals=0
        ),
    )(*(pltpu.with_memory_space_constraint(a, pltpu.HBM) for a in
        (volume.reshape(BLOCK, CELLS), weights, grad_out.reshape(BLOCK, CELLS))))
    conv, gin, gw = pl.pallas_call(
        store,
        out_shape=tuple(jax.ShapeDtypeStruct(a.shape, a.dtype) for a in (conv, gin, gw)),
        in_specs=[vmem, vmem, vmem],
        out_specs=(hbm, hbm, hbm),
        scratch_shapes=[dma((3,))],
    )(*(pltpu.with_memory_space_constraint(a, pltpu.VMEM) for a in (conv, gin, gw)))
    shape = volume.shape
    return conv.reshape(shape), gin.reshape(shape), jnp.transpose(gw, (1, 2, 0))


def solution(mesh):
    return jax.shard_map(
        on_device,
        mesh=mesh,
        in_specs=(P("rep", "chan", "space", None), P(), P("rep", "chan", "space", None)),
        out_specs=(
            P("rep", "chan", "space", None),
            P("rep", "chan", "space", None),
            P(None, None, "chan"),
        ),
        check_vma=False,
    )
```
